256 devices in a mesh: dp: 4 (over z_hi, core), fsdp: 64 (over x, y, z_lo).
Axes of the slice: x: 4, y: 4, z: 8 (z_hi: 2, z_lo: 4; z = z_hi * 4 + z_lo), core: 2. Of those that a mesh axis runs over, the one named last changes fastest.
Arguments:
- inputs: bfloat16 [65536, 8192], P(('dp', 'fsdp')), may hold values from -6 to 6
- cotangent: bfloat16 [65536, 512], P(('dp', 'fsdp')), may hold values from -6 to 6
- old_weight: float32 [512, 8192], P('fsdp'), may hold values from -0.0625 to 0.0625
- old_first: float32 [512, 8192], P('fsdp'), may hold values from -6 to 6
- old_second: float32 [512, 8192], P('fsdp'), may hold values from 0.1 to 2
- holder: int32 [64], replicated, may hold values from 0 to 63, each once
Outputs:
- values: bfloat16 [65536, 512], P(('dp', 'fsdp'))
- grad_input: bfloat16 [65536, 8192], P(('dp', 'fsdp'))
- new_weight: float32 [8192, 512], P('fsdp')
- new_first: float32 [8192, 512], P('fsdp')
- new_second: float32 [8192, 512], P('fsdp')
The draws below stay inside these ranges and needn't reach their ends.
Inputs may be any that keep to these rules, and one draw needn't show every extreme that they name: `holder`: each fsdp position holds a different checkpoint block: every value of 0 to 64 - 1 appears once.
All inputs are finite; a program needn't handle non-finite values.
Results may differ from the reference program's by a relative error of at most 0.0049.
Values may be sent and summed in bfloat16 or wider, within the bound.
A program may use at most 128 MiB of HBM per device.

```python
import math
import jax
import jax.numpy as jnp
from jax import lax

D = 8192
KV = 512
ADAM_STEP = 20
TOKENS = 65536
N_FSDP = 64


def levels(own_key, shape, pieces, smallest, top_value):
    def one(position, shards_of):
        draws = jax.random.uniform(jax.random.fold_in(jax.random.fold_in(own_key, 6), position), (shards_of,), jnp.float32, smallest / len(pieces), top_value / len(pieces))
        return jnp.repeat(jnp.exp(draws), shape[position] // shards_of).reshape((-1,) + (1,) * (len(shape) - position - 1))

    level = one(*pieces[0])
    for cut in pieces[1:]:
        level = level * one(*cut)
    return level


def centred(stream_key, shape, deviation, limit, shards=(), dtype=jnp.bfloat16):
    entries = jax.random.normal(stream_key, shape, jnp.float32) * deviation
    if len(shards) > 0:
        entries = levels(stream_key, shape, shards, -0.22, 0.18) * entries
    return jnp.clip(entries, min=-limit, max=limit).astype(dtype)


def setup_inputs(seed: int = 0) -> dict:
    seeds = jax.random.split(jax.random.key(seed), 7)
    return {
        "inputs": centred(seeds[0], (TOKENS, D), 1.0, 6.0, ((0, 256),)),
        "cotangent": centred(seeds[1], (TOKENS, KV), 1.0, 6.0, ((0, 256),)),
        "old_weight": centred(seeds[2], (KV, D), D ** -0.5, 0.0625, ((0, 64),), jnp.float32),
        "old_first": centred(seeds[3], (KV, D), 1.0, 6.0, ((0, 64),), jnp.float32),
        "old_second": jnp.clip(jnp.exp(math.log(2.0) - 2.9957323 * jax.random.uniform(seeds[4], (KV, D), jnp.float32) ** levels(seeds[4], (KV, D), ((0, 64),), -0.2, 0.2)), 0.1, 2.0),
        "holder": jax.random.permutation(seeds[5], N_FSDP).astype(jnp.int32),
    }


beta_one = 0.9
beta_two = 0.95
epsilon = 1e-08
decay_rate = 0.1
learn_rate = 0.001

def adamw(gradient, weight, first_moment, second_moment):
    first_new = beta_one * first_moment + (1.0 - beta_one) * gradient
    second_new = beta_two * second_moment + (1.0 - beta_two) * gradient * gradient
    corrected = first_new / (1.0 - beta_one ** ADAM_STEP) / (jnp.sqrt(second_new / (1.0 - beta_two ** ADAM_STEP)) + epsilon)
    weight_new = weight - learn_rate * (corrected + decay_rate * weight)
    return (weight_new, first_new, second_new)

def reference(inputs, cotangent, old_weight, old_first, old_second, holder):
    block_order = jnp.argsort(holder).astype(jnp.int32)

    def restore(stored):
        return stored.reshape(N_FSDP, KV // N_FSDP, D)[block_order].reshape(KV, D).T
    weight = restore(old_weight)
    first_moment = restore(old_first)
    second_moment = restore(old_second)
    weight_half = weight.astype(jnp.bfloat16)
    values = jnp.dot(inputs, weight_half, preferred_element_type=jnp.float32).astype(jnp.bfloat16)
    grad_input = lax.dot_general(cotangent, weight_half, (((1,), (1,)), ((), ())), preferred_element_type=jnp.float32).astype(jnp.bfloat16)
    gradient = lax.dot_general(inputs, cotangent, (((0,), (0,)), ((), ())), preferred_element_type=jnp.float32) * TOKENS ** (-0.5)
    new_weight, new_first, new_second = adamw(gradient, weight, first_moment, second_moment)
    return (values, grad_input, new_weight, new_first, new_second)
```

```python
import functools

import jax
import jax.numpy as jnp
from jax import lax
from jax.experimental import pallas as pl
from jax.experimental.pallas import tpu as pltpu
from jax.sharding import PartitionSpec as P

ADAM_STEP = 20
beta_one = 0.9
beta_two = 0.95
epsilon = 1e-08
decay_rate = 0.1
learn_rate = 0.001

MESH = pl.DeviceIdType.MESH
TOK, D, KV = 256, 8192, 512
HALF = KV // 2
PARTS = ((0, 96), (96, 96), (192, 64))
RS_ORDER = ((0, 1, 2), (1, 2, 0), (2, 0, 1))
AG_ORDER = ((2, 1, 0), (0, 2, 1), (1, 0, 2))
MOVE_ORDER = ((0, 1, 2), (1, 2, 0), (2, 0, 1))
XCHUNKS = 4


def device(x, y, z, core):
    return ((z // 4) * 2 + core, x * 16 + y * 4 + lax.rem(z, 4))


def coordinates():
    dp = lax.axis_index("dp")
    f = lax.axis_index("fsdp")
    core = lax.rem(dp, 2)
    return f // 16, lax.rem(f // 4, 4), (dp // 2) * 4 + lax.rem(f, 4), core


def kernel(
    x_hbm, cot_ref, w_ref, f_ref, s_ref, inv_ref,
    val_ref, gin_ref, nw_ref, nf_ref, ns_ref,
    x_own, x_sib, cot_sib, cot_t, grad, gath, wcol, acc,
    rl0, rr0, ha0, hb0, rl1, rr1, ha1, hb1, rl2, rr2, ha2, hb2,
    mid_a, mid_b, mid_c, zsend, zrecv, gfull,
    loc_sem, xs_sem, xr_sem, ag_s, ag_r, sh_s, sh_r, rs_s, rs_r, mv_s, mv_r, fin_s, fin_r,
):
    x, y, z, core = coordinates()
    me = (x, y, lax.rem(z, 4))
    size = (4, 4, 8)
    real = (x, y, z)
    olds = (w_ref, f_ref, s_ref)
    mids = (mid_a, mid_b, mid_c)
    recv = ((rl0, rr0, ha0, hb0), (rl1, rr1, ha1, hb1), (rl2, rr2, ha2, hb2))

    def peer(axis, step):
        at = list(real)
        at[axis] = lax.rem(at[axis] + step + size[axis], size[axis])
        return device(*at, core)

    def slot(axis, step):
        return lax.rem(me[axis] + step + 4, 4)

    sibling = device(x, y, z, 1 - core)
    two = 2 - 4 * lax.rem(z, 2)

    sends = []

    def copy(src, dst, ssem, rsem, to):
        c = pltpu.make_async_remote_copy(
            src_ref=src, dst_ref=dst, send_sem=ssem, recv_sem=rsem, device_id=to, device_id_type=MESH
        )
        c.start()
        sends.append(c)
        return c

    width = D // XCHUNKS
    own = []
    for i in range(XCHUNKS):
        c = pltpu.make_async_copy(
            x_hbm.at[:, pl.ds(i * width, width)], x_own.at[:, pl.ds(i * width, width)], loc_sem.at[i]
        )
        c.start()
        own.append(c)

    bar = pltpu.get_barrier_semaphore()
    greeted = [sibling, peer(2, 4)]
    greeted += [peer(a, d) for a in (0, 1) for d in (1, 2, -1)]
    greeted += [peer(2, d) for d in (1, -1, 2, -2)]
    for to in greeted:
        pl.semaphore_signal(bar, inc=1, device_id=to, device_id_type=MESH)

    mine = w_ref[pl.ds(2 * core, 2)].reshape(HALF, 128)
    gath[me[0], me[1], me[2], pl.ds(core * HALF, HALF), :] = mine.astype(jnp.bfloat16)

    pl.semaphore_wait(bar, len(greeted))

    def ag_view(part, stage, value, low, rows):
        order = AG_ORDER[part]
        idx = [None, None, None]
        for k, axis in enumerate(order):
            idx[axis] = slice(None) if k < stage else (value if k == stage else me[axis])
        return gath.at[idx[0], idx[1], idx[2], pl.ds(core * HALF + PARTS[part][0] + low, rows), :]

    ag = {}

    def ag_send(part, stage):
        axis = AG_ORDER[part][stage]
        rows = PARTS[part][1]
        view = ag_view(part, stage, me[axis], 0, rows)
        ag[part, stage, 0] = copy(view, view, ag_s.at[part, stage, 0], ag_r.at[part, stage, 0], peer(axis, 1))
        ag[part, stage, 1] = copy(view, view, ag_s.at[part, stage, 1], ag_r.at[part, stage, 1], peer(axis, -1))

    def ag_forward(part, stage):
        axis = AG_ORDER[part][stage]
        half = PARTS[part][1] // 2
        ag[part, stage, 0].wait_recv()
        view = ag_view(part, stage, slot(axis, -1), 0, half)
        ag[part, stage, 2] = copy(view, view, ag_s.at[part, stage, 2], ag_r.at[part, stage, 2], peer(axis, 1))
        ag[part, stage, 1].wait_recv()
        view = ag_view(part, stage, slot(axis, 1), half, half)
        ag[part, stage, 3] = copy(view, view, ag_s.at[part, stage, 3], ag_r.at[part, stage, 3], peer(axis, -1))

    def ag_finish(part, stage):
        ag[part, stage, 2].wait_recv()
        ag[part, stage, 3].wait_recv()

    share = {}

    def ag_share(part):
        view = gath.at[:, :, :, pl.ds(core * HALF + PARTS[part][0], PARTS[part][1]), :]
        share[part] = copy(view, view, sh_s.at[part], sh_r.at[part], sibling)

    mv = {}

    def mv_view(n, stage, value):
        axis = MOVE_ORDER[n][stage]
        if stage == 0:
            idx = [slice(None)] * 3
            idx[axis] = value
            return olds[n].at[idx[0], idx[1], idx[2]]
        if stage == 1:
            rest = [a for a in range(3) if a != MOVE_ORDER[n][0]]
            if rest[0] == axis:
                return mids[n].at[0, :, value]
            return mids[n].at[0, :, :, value]
        return mids[n].at[1, :, :, value]

    def mv_send(n, stage):
        axis = MOVE_ORDER[n][stage]
        for k, step in enumerate((1, -1, 2)):
            far = two if (axis == 2 and step == 2) else step
            mv[n, stage, k] = copy(
                mv_view(n, stage, slot(axis, step)), mids[n].at[stage, me[axis]],
                mv_s.at[n, stage, k], mv_r.at[n, stage, k], peer(axis, far),
            )
        mids[n][stage, me[axis]] = mv_view(n, stage, me[axis])[...]

    def mv_finish(n, stage):
        for k in range(3):
            mv[n, stage, k].wait_recv()

    rs = {}

    def rs_view(part, stage, value, low, rows):
        order = RS_ORDER[part]
        idx = [None, None, None]
        for k, axis in enumerate(order):
            idx[axis] = me[axis] if k < stage else (value if k == stage else slice(None))
        return grad.at[idx[0], idx[1], idx[2], pl.ds(PARTS[part][0] + low, rows), :]

    def rs_buf(part, which, stage, low, rows):
        ref = recv[part][which]
        if stage == 0:
            return ref.at[:, pl.ds(0, 4), pl.ds(low, rows), :]
        if stage == 1:
            return ref.at[:, 4, pl.ds(low, rows), :]
        return ref.at[0, 5, pl.ds(low, rows), :]

    def rs_copy(part, stage, k, value, low, rows, which, at, step):
        axis = RS_ORDER[part][stage]
        rs[part, stage, k] = copy(
            rs_view(part, stage, value, low, rows), rs_buf(part, which, stage, at, rows),
            rs_s.at[part, stage, k], rs_r.at[part, stage, k], peer(axis, step),
        )

    def rs_send(part, stage):
        axis = RS_ORDER[part][stage]
        half = PARTS[part][1] // 2
        opposite, right, left = slot(axis, 2), slot(axis, 1), slot(axis, -1)
        rs_copy(part, stage, 0, opposite, 0, half, 2, 0, 1)
        rs_copy(part, stage, 1, opposite, half, half, 3, 0, -1)
        rs_copy(part, stage, 2, right, half, half, 0, half, 1)
        rs_copy(part, stage, 3, left, 0, half, 1, 0, -1)

    def add(view, *others):
        total = view[...].astype(jnp.float32)
        for o in others:
            total = total + o[...].astype(jnp.float32)
        return total.astype(jnp.bfloat16)

    def rs_forward(part, stage):
        axis = RS_ORDER[part][stage]
        half = PARTS[part][1] // 2
        right, left = slot(axis, 1), slot(axis, -1)
        rs[part, stage, 0].wait_recv()
        view = rs_view(part, stage, right, 0, half)
        view[...] = add(view, rs_buf(part, 2, stage, 0, half))
        rs_copy(part, stage, 4, right, 0, half, 0, 0, 1)
        rs[part, stage, 1].wait_recv()
        view = rs_view(part, stage, left, half, half)
        view[...] = add(view, rs_buf(part, 3, stage, 0, half))
        rs_copy(part, stage, 5, left, half, half, 1, half, -1)

    def rs_finish(part, stage):
        axis = RS_ORDER[part][stage]
        rows = PARTS[part][1]
        for k in (2, 3, 4, 5):
            rs[part, stage, k].wait_recv()
        view = rs_view(part, stage, me[axis], 0, rows)
        total = add(view, rs_buf(part, 0, stage, 0, rows), rs_buf(part, 1, stage, 0, rows))
        if stage < 2:
            view[...] = total
        else:
            zsend[pl.ds(PARTS[part][0], rows), :] = total
            rs[part, 3] = copy(
                zsend.at[pl.ds(PARTS[part][0], rows), :], zrecv.at[pl.ds(PARTS[part][0], rows), :],
                fin_s.at[part], fin_r.at[part], peer(2, 4),
            )

    for part in range(3):
        ag_send(part, 0)
    cot_copy = copy(
        cot_ref.at[:, pl.ds(pl.multiple_of((1 - core) * HALF, HALF), HALF)], cot_sib,
        xs_sem.at[XCHUNKS], xr_sem.at[XCHUNKS], sibling,
    )
    xcopy = []
    for i in range(XCHUNKS):
        xcopy.append(
            copy(
                x_hbm.at[:, pl.ds(i * width, width)], x_sib.at[:, pl.ds(i * width, width)],
                xs_sem.at[i], xr_sem.at[i], sibling,
            )
        )
    for n in range(3):
        mv_send(n, 0)
    for part in range(3):
        ag_forward(part, 0)
    cot_copy.wait_recv()
    cot_half = cot_ref[:, pl.ds(pl.multiple_of(core * HALF, HALF), HALF)]
    cot_t[:, pl.ds(0, TOK)] = cot_half.astype(jnp.float32).T.astype(jnp.bfloat16)
    cot_t[:, pl.ds(TOK, TOK)] = cot_sib[...].astype(jnp.float32).T.astype(jnp.bfloat16)
    for part in range(3):
        ag_finish(part, 0)
        ag_send(part, 1)

    def grad_chunk(i):
        at = pl.ds(pl.multiple_of(i * 512, 512), 512)
        total = jnp.dot(cot_t[:, pl.ds(0, TOK)], x_own[:, at], preferred_element_type=jnp.float32)
        total = total + jnp.dot(cot_t[:, pl.ds(TOK, TOK)], x_sib[:, at], preferred_element_type=jnp.float32)
        total = (total * (1.0 / 256.0)).astype(jnp.bfloat16)
        for k in range(4):
            grad[i // 4, lax.rem(i, 4), k] = total[:, k * 128:(k + 1) * 128]

    def grad_span(first, last):
        def body(i, carry):
            grad_chunk(i)
            return carry

        lax.fori_loop(first, last, body, 0)

    for i in range(2):
        own[i].wait()
        xcopy[i].wait_recv()
        grad_span(4 * i, 4 * i + 4)
    for part in range(3):
        ag_forward(part, 1)
    for n in range(3):
        mv_finish(n, 0)
        mv_send(n, 1)
    for i in range(2, 4):
        own[i].wait()
        xcopy[i].wait_recv()
        grad_span(4 * i, 4 * i + 4)
    for part in range(3):
        ag_finish(part, 1)
        ag_send(part, 2)
    for part in range(3):
        rs_send(part, 0)
    for n in range(3):
        mv_finish(n, 1)
        mv_send(n, 2)
    for part in range(3):
        ag_forward(part, 2)
    for part in range(3):
        rs_forward(part, 0)
    for part in range(3):
        ag_finish(part, 2)
        ag_share(part)
    for part in range(3):
        rs_finish(part, 0)
        rs_send(part, 1)
    for part in range(3):
        share[part].wait_recv()

    acc[...] = jnp.zeros_like(acc)

    def block(i):
        p = inv_ref[i]
        return p // 16, lax.rem(p // 4, 4), lax.rem(p, 4)

    def project(t, carry):
        rows = pl.ds(pl.multiple_of(t * 32, 32), 32)
        for k in range(32):
            a = block(2 * k)
            b = block(2 * k + 1)
            first = gath[a[0], a[1], a[2], rows, :].astype(jnp.float32).reshape(4, 8, 128)
            second = gath[b[0], b[1], b[2], rows, :].astype(jnp.float32).reshape(4, 8, 128)
            both = jnp.concatenate([first, second], axis=1).astype(jnp.bfloat16)
            for j in range(4):
                wcol[pl.ds(16 * k, 16), pl.ds(128 * j, 128)] = both[j]
        at = pl.ds(pl.multiple_of(t * 512, 512), 512)
        acc[...] += lax.dot_general(
            x_own[:, at], wcol[...], (((1,), (1,)), ((), ())), preferred_element_type=jnp.float32
        )
        gin_ref[:, at] = jnp.dot(cot_ref[...], wcol[...], preferred_element_type=jnp.float32).astype(
            jnp.bfloat16
        )
        return carry

    lax.fori_loop(0, 8, project, 0)
    for part in range(3):
        rs_forward(part, 1)
    lax.fori_loop(8, 16, project, 0)
    val_ref[...] = acc[...].astype(jnp.bfloat16)
    for part in range(3):
        rs_finish(part, 1)
        rs_send(part, 2)
    for n in range(3):
        mv_finish(n, 2)
    for part in range(3):
        rs_forward(part, 2)
    for part in range(3):
        rs_finish(part, 2)
    for part in range(3):
        rs[part, 3].wait_recv()
    half_rows = pl.ds(pl.multiple_of(core * HALF, HALF), HALF)
    gfull[half_rows, :] = zsend[...].astype(jnp.float32) + zrecv[...].astype(jnp.float32)
    last = copy(gfull.at[half_rows, :], gfull.at[half_rows, :], fin_s.at[3], fin_r.at[3], sibling)
    last.wait_recv()

    def restored(n):
        order = MOVE_ORDER[n]
        rows = []
        for i in range(64):
            p = block(i)
            rows.append(mids[n][2, p[order[2]], p[order[1]], p[order[0]]])
        return jnp.concatenate(rows, axis=0)

    gradient = gfull[...]
    weight = restored(0)
    first_new = beta_one * restored(1) + (1.0 - beta_one) * gradient
    second_new = beta_two * restored(2) + (1.0 - beta_two) * gradient * gradient
    corrected = (
        first_new
        / (1.0 - beta_one**ADAM_STEP)
        / (jnp.sqrt(second_new / (1.0 - beta_two**ADAM_STEP)) + epsilon)
    )
    weight_new = weight - learn_rate * (corrected + decay_rate * weight)
    nw_ref[...] = weight_new.T
    nf_ref[...] = first_new.T
    ns_ref[...] = second_new.T

    for c in sends:
        c.wait_send()


def on_device(inputs, cotangent, old_weight, old_first, old_second, holder):
    slots = jnp.arange(64, dtype=jnp.int32)
    inverse = jnp.sum(jnp.where(holder[None, :] == slots[:, None], slots[None, :], 0), axis=1)

    def tiles(a):
        return a.reshape(8, 64, 128).transpose(1, 0, 2).reshape(4, 4, 4, 8, 128)

    bf, f32 = jnp.bfloat16, jnp.float32
    vmem = pl.BlockSpec(memory_space=pltpu.VMEM)
    dma = pltpu.SemaphoreType.DMA
    buffers = []
    for _, rows in PARTS:
        buffers += [pltpu.VMEM((4, 6, rows, 128), bf)] * 2 + [pltpu.VMEM((4, 6, rows // 2, 128), bf)] * 2
    return pl.pallas_call(
        kernel,
        out_shape=(
            jax.ShapeDtypeStruct((TOK, KV), bf),
            jax.ShapeDtypeStruct((TOK, D), bf),
            jax.ShapeDtypeStruct((128, KV), f32),
            jax.ShapeDtypeStruct((128, KV), f32),
            jax.ShapeDtypeStruct((128, KV), f32),
        ),
        in_specs=[pl.BlockSpec(memory_space=pl.ANY)] + [vmem] * 4 + [pl.BlockSpec(memory_space=pltpu.SMEM)],
        out_specs=(vmem,) * 5,
        scratch_shapes=[
            pltpu.VMEM((TOK, D), bf),
            pltpu.VMEM((TOK, D), bf),
            pltpu.VMEM((TOK, HALF), bf),
            pltpu.VMEM((HALF, 2 * TOK), bf),
            pltpu.VMEM((4, 4, 4, HALF, 128), bf),
            pltpu.VMEM((4, 4, 4, KV, 128), bf),
            pltpu.VMEM((KV, 512), bf),
            pltpu.VMEM((TOK, KV), f32),
            *buffers,
            *[pltpu.VMEM((3, 4, 4, 4, 8, 128), f32)] * 3,
            pltpu.VMEM((HALF, 128), bf),
            pltpu.VMEM((HALF, 128), bf),
            pltpu.VMEM((KV, 128), f32),
            dma((XCHUNKS,)),
            dma((XCHUNKS + 1,)),
            dma((XCHUNKS + 1,)),
            dma((3, 3, 4)),
            dma((3, 3, 4)),
            dma((3,)),
            dma((3,)),
            dma((3, 3, 6)),
            dma((3, 3, 6)),
            dma((3, 3, 3)),
            dma((3, 3, 3)),
            dma((4,)),
            dma((4,)),
        ],
        compiler_params=pltpu.CompilerParams(
            collective_id=0, has_side_effects=True, vmem_limit_bytes=58 * 2**20
        ),
    )(inputs, cotangent, tiles(old_weight), tiles(old_first), tiles(old_second), inverse)


def solution(mesh):
    rows = P(("dp", "fsdp"), None)
    shard = P("fsdp", None)
    return jax.shard_map(
        on_device,
        mesh=mesh,
        in_specs=(rows, rows, shard, shard, shard, P()),
        out_specs=(rows, rows, shard, shard, shard),
        check_vma=False,
    )
```

```python
import functools

import jax
import jax.numpy as jnp
from jax import lax
from jax.experimental import pallas as pl
from jax.experimental.pallas import tpu as pltpu
from jax.sharding import PartitionSpec as P

ADAM_STEP = 20
beta_one = 0.9
beta_two = 0.95
epsilon = 1e-08
decay_rate = 0.1
learn_rate = 0.001

MESH = pl.DeviceIdType.MESH
TOK, D, KV = 256, 8192, 512
HALF = KV // 2
PARTS = ((0, 96), (96, 96), (192, 64))
RS_ORDER = ((0, 1, 2), (1, 2, 0), (2, 0, 1))
AG_ORDER = ((2, 1, 0), (0, 2, 1), (1, 0, 2))
MOVE_ORDER = ((0, 1, 2), (1, 2, 0), (2, 0, 1))
XCHUNKS = 4


def device(x, y, z, core):
    return ((z // 4) * 2 + core, x * 16 + y * 4 + lax.rem(z, 4))


def coordinates():
    dp = lax.axis_index("dp")
    f = lax.axis_index("fsdp")
    core = lax.rem(dp, 2)
    return f // 16, lax.rem(f // 4, 4), (dp // 2) * 4 + lax.rem(f, 4), core


def kernel(
    x_hbm, cot_hbm, w_hbm, f_hbm, s_hbm, holder_ref,
    val_ref, gin_ref, gfull, new_a, new_b, new_c,
    cot_ref, w_ref, f_ref, s_ref, x_own, x_sib, cot_sib, cot_t, grad, gath, pair, order_ref, cot_sur, acc,
    in_0, in_1, in_2, next_0, next_1, next_2, last_in,
    mid_a, mid_b, mid_c, zsend, zrecv,
    loc_sem, pair_s, pair_r, xs_sem, xr_sem, ag_s, ag_r, ag2_s, ag2_r, sh_s, sh_r,
    rs0_s, rs0_r, rs_s, rs_r, mv_s, mv_r, ms_s, ms_r, fin_s, fin_r,
):
    x, y, z, core = coordinates()
    real = (x, y, z)
    size = (4, 4, 8)
    me = (x, y, lax.rem(z, 4))
    olds = (w_ref, f_ref, s_ref)
    mids = (mid_a, mid_b, mid_c)
    news = (new_a, new_b, new_c)
    first_in = (in_0, in_1, in_2)
    second_in = (next_0, next_1, next_2)

    def peer(axis, step):
        at = list(real)
        at[axis] = lax.rem(at[axis] + step + size[axis], size[axis])
        return device(*at, core)

    def slot(axis, step):
        return lax.rem(me[axis] + step + 4, 4)

    sibling = device(x, y, z, 1 - core)
    two = 2 - 4 * lax.rem(z, 2)
    sends = []

    def plan(src, dst, ssem, rsem, to):
        return pltpu.make_async_remote_copy(
            src_ref=src, dst_ref=dst, send_sem=ssem, recv_sem=rsem, device_id=to, device_id_type=MESH
        )

    def copy(src, dst, ssem, rsem, to):
        c = plan(src, dst, ssem, rsem, to)
        c.start()
        sends.append(c)
        return c

    small = []
    for i, (src, dst) in enumerate(((w_hbm, w_ref), (cot_hbm, cot_ref), (f_hbm, f_ref), (s_hbm, s_ref))):
        c = pltpu.make_async_copy(src, dst, loc_sem.at[XCHUNKS + i])
        c.start()
        small.append(c)
    width = D // XCHUNKS
    own = []
    for i in range(XCHUNKS):
        c = pltpu.make_async_copy(
            x_hbm.at[:, pl.ds(i * width, width)], x_own.at[:, pl.ds(i * width, width)], loc_sem.at[i]
        )
        c.start()
        own.append(c)

    bar = pltpu.get_barrier_semaphore()
    greeted = [sibling, peer(2, 4)]
    greeted += [peer(a, d) for a in (0, 1) for d in (1, 2, -1)]
    greeted += [peer(2, d) for d in (1, -1, 2, -2)]
    for to in greeted:
        pl.semaphore_signal(bar, inc=1, device_id=to, device_id_type=MESH)

    small[0].wait()
    pl.semaphore_wait(bar, len(greeted))

    def ag_view(part, at, low, rows):
        if isinstance(at[2], slice):
            pairs, member = at[2], at[2]
        else:
            pairs, member = at[2] // 2, lax.rem(at[2], 2)
        return gath.at[at[0], at[1], pairs, member, pl.ds(core * HALF + PARTS[part][0] + low, rows), :]

    ag = {}

    def ag_send(part, stage):
        order = AG_ORDER[part]
        axis = order[stage]
        rows = PARTS[part][1]
        half = rows // 2
        at = list(me)
        for a in order[:stage]:
            at[a] = slice(None)
        for k, (step, low, n) in enumerate(((1, 0, rows), (-1, 0, rows), (2, 0, half), (-2, half, half))):
            view = ag_view(part, at, low, n)
            ag[part, stage, k] = copy(
                view, view, ag_s.at[part, stage, k], ag_r.at[part, stage, k], peer(axis, step)
            )

    def ag_finish(part, stage):
        for k in range(4):
            ag[part, stage, k].wait_recv()

    def ag2_at(part, value):
        at = [slice(None)] * 3
        at[AG_ORDER[part][2]] = value
        return at

    def ag2_send(part):
        axis = AG_ORDER[part][2]
        view = ag_view(part, ag2_at(part, me[axis]), 0, PARTS[part][1])
        for k, step in enumerate((1, -1)):
            ag[part, 2, k] = copy(view, view, ag2_s.at[part, k], ag2_r.at[part, k], peer(axis, step))

    def ag2_forward(part):
        axis = AG_ORDER[part][2]
        half = PARTS[part][1] // 2
        for k, (step, low) in enumerate(((1, 0), (-1, half))):
            ag[part, 2, k].wait_recv()
            view = ag_view(part, ag2_at(part, slot(axis, -step)), low, half)
            ag[part, 2, 2 + k] = copy(view, view, ag2_s.at[part, 2 + k], ag2_r.at[part, 2 + k], peer(axis, step))

    def ag2_finish(part):
        ag[part, 2, 2].wait_recv()
        ag[part, 2, 3].wait_recv()

    share = {}

    def ag_share(part):
        view = ag_view(part, (slice(None),) * 3, 0, PARTS[part][1])
        share[part] = copy(view, view, sh_s.at[part], sh_r.at[part], sibling)

    mv = {}
    active = [lax.rem(me[MOVE_ORDER[n][2]], 2) == core for n in range(3)]

    def mv_view(n, stage, value):
        axis = MOVE_ORDER[n][stage]
        if stage == 0:
            idx = [slice(None)] * 3
            idx[axis] = value
            return olds[n].at[idx[0], idx[1], idx[2]]
        if stage == 1:
            rest = [a for a in range(3) if a != MOVE_ORDER[n][0]]
            if rest[0] == axis:
                return mids[n].at[0, :, value]
            return mids[n].at[0, :, :, value]
        return mids[n].at[1, :, :, value]

    def mv_dst(n, stage, value):
        return news[n].at[value] if stage == 2 else mids[n].at[stage, value]

    def mv_send(n, stage):
        axis = MOVE_ORDER[n][stage]
        for k, step in enumerate((1, -1, 2)):
            far = two if (axis == 2 and step == 2) else step
            mv[n, stage, k] = plan(
                mv_view(n, stage, slot(axis, step)), mv_dst(n, stage, me[axis]),
                mv_s.at[n, stage, k], mv_r.at[n, stage, k], peer(axis, far),
            )
        home = mv_dst(n, stage, me[axis])
        here = mv_view(n, stage, me[axis])

        @pl.when(active[n])
        def _():
            for k in range(3):
                mv[n, stage, k].start()
            home[...] = here[...]

    def mv_finish(n, stage):
        @pl.when(active[n])
        def _():
            for k in range(3) if stage < 2 else (2,):
                mv[n, stage, k].wait_recv()

        if stage == 2:
            @pl.when(jnp.logical_not(active[n]))
            def _():
                mv[n, stage, 0].wait_recv()
                mv[n, stage, 1].wait_recv()

    def mv_share(n):
        for k in range(2):
            view = news[n].at[core + 2 * k]
            mv[n, 3, k] = copy(view, view, ms_s.at[n, k], ms_r.at[n, k], sibling)

    rs = {}

    def rs_view(part, stage, value, low, rows):
        order = RS_ORDER[part]
        at = [me[0], me[1], me[2]]
        at[order[stage]] = value
        for a in order[stage + 1:]:
            at[a] = slice(None)
        return grad.at[at[0], at[1], at[2], pl.ds(PARTS[part][0] + low, rows), :]

    def rs_buf(part, stage, which, low, rows):
        if stage == 0:
            return first_in[part].at[which, :, :, pl.ds(low, rows), :]
        if stage == 1:
            return second_in[part].at[which, :, pl.ds(low, rows), :]
        return last_in.at[which, pl.ds(PARTS[part][0] + low, rows), :]

    def rs0_copy(part, k, value, low, rows, which, step):
        axis = RS_ORDER[part][0]
        rs[part, 0, k] = copy(
            rs_view(part, 0, value, low, rows), rs_buf(part, 0, which, low, rows),
            rs0_s.at[part, k], rs0_r.at[part, k], peer(axis, step),
        )

    def rs0_far(part):
        axis = RS_ORDER[part][0]
        half = PARTS[part][1] // 2
        rs0_copy(part, 0, slot(axis, 2), 0, half, 2, 1)
        rs0_copy(part, 1, slot(axis, 2), half, half, 2, -1)

    def rs0_near(part):
        axis = RS_ORDER[part][0]
        half = PARTS[part][1] // 2
        rs0_copy(part, 2, slot(axis, 1), half, half, 0, 1)
        rs0_copy(part, 3, slot(axis, -1), 0, half, 1, -1)

    def add(view, *others):
        total = view[...].astype(jnp.float32)
        for o in others:
            total = total + o[...].astype(jnp.float32)
        return total.astype(jnp.bfloat16)

    def rs0_forward(part):
        axis = RS_ORDER[part][0]
        half = PARTS[part][1] // 2
        for k, (step, low) in enumerate(((1, 0), (-1, half))):
            value = slot(axis, step)
            rs[part, 0, k].wait_recv()
            for i in range(4):
                view = rs_view(part, 0, value, low, half).at[i]
                view[...] = add(view, rs_buf(part, 0, 2, low, half).at[i])
            rs0_copy(part, 4 + k, value, low, half, k, step)

    def rs_copy(part, stage, k, value, low, rows, which, step):
        axis = RS_ORDER[part][stage]
        rs[part, stage, k] = copy(
            rs_view(part, stage, value, low, rows), rs_buf(part, stage, which, low, rows),
            rs_s.at[part, stage - 1, k], rs_r.at[part, stage - 1, k], peer(axis, step),
        )

    def rs_send(part, stage):
        axis = RS_ORDER[part][stage]
        rows = PARTS[part][1]
        half = rows // 2
        rs_copy(part, stage, 0, slot(axis, 1), 0, rows, 0, 1)
        rs_copy(part, stage, 1, slot(axis, -1), 0, rows, 1, -1)
        rs_copy(part, stage, 2, slot(axis, 2), 0, half, 2, 2)
        rs_copy(part, stage, 3, slot(axis, 2), half, half, 2, -2)

    def rs0_finish(part):
        axis = RS_ORDER[part][0]
        rows = PARTS[part][1]
        for k in (2, 3, 4, 5):
            rs[part, 0, k].wait_recv()
        for i in range(4):
            view = rs_view(part, 0, me[axis], 0, rows).at[i]
            view[...] = add(view, *[rs_buf(part, 0, which, 0, rows).at[i] for which in range(2)])
        rs_send(part, 1)

    def rs_finish(part, stage):
        rows = PARTS[part][1]
        for k in range(4):
            rs[part, stage, k].wait_recv()
        view = rs_view(part, stage, me[RS_ORDER[part][stage]], 0, rows)
        total = add(view, *[rs_buf(part, stage, which, 0, rows) for which in range(3)])
        if stage == 1:
            view[...] = total
            rs_send(part, 2)
        else:
            lines = pl.ds(PARTS[part][0], rows)
            zsend[lines, :] = total
            rs[part, 3] = copy(
                zsend.at[lines, :], zrecv.at[lines, :], fin_s.at[part], fin_r.at[part], peer(2, 4)
            )

    def grad_chunk(i, carry):
        at = pl.ds(pl.multiple_of(i * 512, 512), 512)
        total = jnp.dot(cot_t[:, pl.ds(0, TOK)], x_own[:, at], preferred_element_type=jnp.float32)
        total = total + jnp.dot(cot_t[:, pl.ds(TOK, TOK)], x_sib[:, at], preferred_element_type=jnp.float32)
        total = (total * (1.0 / 256.0)).astype(jnp.bfloat16)
        for k in range(4):
            grad[i // 4, lax.rem(i, 4), k] = total[:, k * 128:(k + 1) * 128]
        return carry

    def project(t, carry):
        rows = pl.ds(pl.multiple_of((t // 8) * HALF + lax.rem(t, 4) * 64, 64), 64)
        tiles = gath[:, :, :, lax.rem(t // 4, 2), rows, :]
        columns = jnp.concatenate(
            [tiles[:, :, :, 16 * j:16 * j + 16, :].reshape(KV, 128) for j in range(4)], axis=1
        )
        at = pl.ds(pl.multiple_of(t * 512, 512), 512)
        acc[...] += lax.dot_general(
            x_own[:, at], columns, (((1,), (1,)), ((), ())), preferred_element_type=jnp.float32
        )
        gin_ref[:, at] = jnp.dot(cot_sur[...], columns, preferred_element_type=jnp.float32).astype(
            jnp.bfloat16
        )
        return carry

    parity = lax.rem(z, 2)
    pair_copy = copy(
        w_ref.at[2 * core + 1 - parity], pair, pair_s.at[0], pair_r.at[0], peer(2, 1 - 2 * parity)
    )
    for c in small[1:]:
        c.wait()
    cot_copy = copy(
        cot_ref.at[:, pl.ds(pl.multiple_of((1 - core) * HALF, HALF), HALF)], cot_sib,
        xs_sem.at[XCHUNKS], xr_sem.at[XCHUNKS], sibling,
    )
    for n in range(3):
        mv_send(n, 0)
    xcopy = []
    for i in range(XCHUNKS):
        xcopy.append(
            copy(
                x_hbm.at[:, pl.ds(i * width, width)], x_sib.at[:, pl.ds(i * width, width)],
                xs_sem.at[i], xr_sem.at[i], sibling,
            )
        )
    mine = w_ref[2 * core + parity].reshape(16, 8, 128)
    pair_copy.wait_recv()
    other = pair[...].reshape(16, 8, 128)
    both = jnp.concatenate(
        [jnp.where(parity == 0, mine, other), jnp.where(parity == 0, other, mine)], axis=1
    )
    gath[me[0], me[1], me[2] // 2, parity, pl.ds(core * HALF, HALF), :] = both.reshape(HALF, 128).astype(
        jnp.bfloat16
    )
    for part in range(3):
        ag_send(part, 0)
    lane_block = lax.broadcasted_iota(jnp.int32, (1, KV), 1) // 8
    target = lax.rem(lax.broadcasted_iota(jnp.int32, (1, KV), 1), 8)
    for p in range(64):
        target = jnp.where(lane_block == p, target + 8 * holder_ref[p], target)
    hit = lax.broadcasted_iota(jnp.int32, (KV, KV), 0) == target
    order_ref[...] = jnp.where(hit, 1.0, 0.0).astype(jnp.bfloat16)
    cot_sur[...] = jnp.dot(cot_ref[...], order_ref[...], preferred_element_type=jnp.float32).astype(jnp.bfloat16)
    for part in range(3):
        ag_finish(part, 0)
        ag_send(part, 1)
    cot_copy.wait_recv()
    cot_half = cot_ref[:, pl.ds(pl.multiple_of(core * HALF, HALF), HALF)]
    cot_t[:, pl.ds(0, TOK)] = cot_half.astype(jnp.float32).T.astype(jnp.bfloat16)
    cot_t[:, pl.ds(TOK, TOK)] = cot_sib[...].astype(jnp.float32).T.astype(jnp.bfloat16)
    for n in range(3):
        mv_finish(n, 0)
        mv_send(n, 1)
    for part in range(3):
        ag_finish(part, 1)
        ag2_send(part)
    for i in range(XCHUNKS):
        own[i].wait()
        xcopy[i].wait_recv()
        lax.fori_loop(4 * i, 4 * i + 4, grad_chunk, 0)
    for part in range(3):
        rs0_far(part)
    for n in range(3):
        mv_finish(n, 1)
        mv_send(n, 2)
    for part in range(3):
        rs0_near(part)
    for part in range(3):
        ag2_forward(part)
    for part in range(3):
        rs0_forward(part)
    for part in range(3):
        ag2_finish(part)
        ag_share(part)
    acc[...] = jnp.zeros_like(acc)
    for part in range(3):
        share[part].wait_recv()
    lax.fori_loop(0, 8, project, 0)
    for part in range(3):
        rs0_finish(part)
    for n in range(3):
        mv_finish(n, 2)
        mv_share(n)
    lax.fori_loop(8, 16, project, 0)
    for part in range(3):
        rs_finish(part, 1)
    val_ref[...] = lax.dot_general(
        acc[...].astype(jnp.bfloat16), order_ref[...], (((1,), (1,)), ((), ())),
        preferred_element_type=jnp.float32,
    ).astype(jnp.bfloat16)
    for part in range(3):
        rs_finish(part, 2)
    for n in range(3):
        mv[n, 3, 0].wait_recv()
        mv[n, 3, 1].wait_recv()
    for part in range(3):
        rs[part, 3].wait_recv()
    half_rows = pl.ds(pl.multiple_of(core * HALF, HALF), HALF)
    gfull[half_rows, :] = zsend[...].astype(jnp.float32) + zrecv[...].astype(jnp.float32)
    last = copy(gfull.at[half_rows, :], gfull.at[half_rows, :], fin_s.at[3], fin_r.at[3], sibling)
    last.wait_recv()
    for n in range(3):
        @pl.when(active[n])
        def _(n=n):
            for stage in range(3):
                for k in range(3):
                    mv[n, stage, k].wait_send()
    for c in sends:
        c.wait_send()


def update_kernel(
    holder_ref, val_ref, gin_ref, grad_ref, w_ref, f_ref, s_ref, val_out, gin_out, nw_ref, nf_ref, ns_ref, weight_ref, first_ref, second_ref, sem
):
    copies = [
        pltpu.make_async_copy(gin_ref, gin_out, sem.at[0]),
        pltpu.make_async_copy(val_ref, val_out, sem.at[1]),
    ]
    for c in copies:
        c.start()

    targets = (weight_ref, first_ref, second_ref)
    for p in range(64):
        at = (p // 16, (p // 4) % 4, p % 4)
        rows = pl.ds(pl.multiple_of(holder_ref[p] * 8, 8), 8)
        for ref, order, out in zip((w_ref, f_ref, s_ref), MOVE_ORDER, targets):
            out[rows, :] = ref[at[order[2]], at[order[1]], at[order[0]]]
    gradient = grad_ref[...]
    weight = weight_ref[...]
    first_new = beta_one * first_ref[...] + (1.0 - beta_one) * gradient
    second_new = beta_two * second_ref[...] + (1.0 - beta_two) * gradient * gradient
    corrected = (
        first_new
        / (1.0 - beta_one**ADAM_STEP)
        / (jnp.sqrt(second_new / (1.0 - beta_two**ADAM_STEP)) + epsilon)
    )
    nw_ref[...] = (weight - learn_rate * (corrected + decay_rate * weight)).T
    nf_ref[...] = first_new.T
    ns_ref[...] = second_new.T
    for c in copies:
        c.wait()


def on_device(inputs, cotangent, old_weight, old_first, old_second, holder):
    def tiles(a):
        return a.reshape(8, 64, 128).transpose(1, 0, 2).reshape(4, 4, 4, 8, 128)

    bf, f32 = jnp.bfloat16, jnp.float32
    vmem = pl.BlockSpec(memory_space=pltpu.VMEM)
    smem = pl.BlockSpec(memory_space=pltpu.SMEM)
    anywhere = pl.BlockSpec(memory_space=pl.ANY)
    hbm = pl.BlockSpec(memory_space=pltpu.HBM)
    dma = pltpu.SemaphoreType.DMA
    state = (4, 4, 4, 8, 128)
    parts = pl.pallas_call(
        kernel,
        out_shape=(
            pltpu.VMEM((TOK, KV), bf),
            pltpu.VMEM((TOK, D), bf),
            pltpu.VMEM((KV, 128), f32),
            pltpu.VMEM(state, f32),
            pltpu.VMEM(state, f32),
            pltpu.VMEM(state, f32),
        ),
        in_specs=[hbm] * 5 + [smem],
        out_specs=(vmem,) * 6,
        scratch_shapes=[
            pltpu.VMEM((TOK, KV), bf),
            *[pltpu.VMEM(state, f32)] * 3,
            pltpu.VMEM((TOK, D), bf),
            pltpu.VMEM((TOK, D), bf),
            pltpu.VMEM((TOK, HALF), bf),
            pltpu.VMEM((HALF, 2 * TOK), bf),
            pltpu.VMEM((4, 4, 4, HALF, 128), bf),
            pltpu.VMEM((4, 4, 2, 2, KV, 128), bf),
            pltpu.VMEM((4, 4, 8, 128), f32),
            pltpu.VMEM((KV, KV), bf),
            pltpu.VMEM((TOK, KV), bf),
            pltpu.VMEM((TOK, KV), f32),
            *[pltpu.VMEM((3, 4, 4, rows, 128), bf) for _, rows in PARTS],
            *[pltpu.VMEM((3, 4, rows, 128), bf) for _, rows in PARTS],
            pltpu.VMEM((3, HALF, 128), bf),
            *[pltpu.VMEM((2,) + (4, 4, 4, 8, 128), f32)] * 3,
            pltpu.VMEM((HALF, 128), bf),
            pltpu.VMEM((HALF, 128), bf),
            dma((XCHUNKS + 4,)),
            dma((1,)),
            dma((1,)),
            dma((XCHUNKS + 1,)),
            dma((XCHUNKS + 1,)),
            dma((3, 2, 4)),
            dma((3, 2, 4)),
            dma((3, 4)),
            dma((3, 4)),
            dma((3,)),
            dma((3,)),
            dma((3, 6)),
            dma((3, 6)),
            dma((3, 2, 4)),
            dma((3, 2, 4)),
            dma((3, 3, 3)),
            dma((3, 3, 3)),
            dma((3, 2)),
            dma((3, 2)),
            dma((4,)),
            dma((4,)),
        ],
        compiler_params=pltpu.CompilerParams(
            collective_id=0, has_side_effects=True, vmem_limit_bytes=117 * 2**19
        ),
    )(inputs, cotangent, tiles(old_weight), tiles(old_first), tiles(old_second), holder)
    values, grad_input, gradient, weight, first, second = parts
    shard = jax.ShapeDtypeStruct((128, KV), f32)
    return pl.pallas_call(
        update_kernel,
        out_shape=(
            jax.ShapeDtypeStruct((TOK, KV), bf),
            jax.ShapeDtypeStruct((TOK, D), bf),
            shard,
            shard,
            shard,
        ),
        in_specs=[smem] + [vmem] * 6,
        out_specs=(anywhere, anywhere, vmem, vmem, vmem),
        scratch_shapes=[pltpu.VMEM((KV, 128), f32)] * 3 + [dma((2,))],
        compiler_params=pltpu.CompilerParams(vmem_limit_bytes=16 * 2**20),
    )(holder, values, grad_input, gradient, weight, first, second)


def solution(mesh):
    rows = P(("dp", "fsdp"), None)
    shard = P("fsdp", None)
    return jax.shard_map(
        on_device,
        mesh=mesh,
        in_specs=(rows, rows, shard, shard, shard, P()),
        out_specs=(rows, rows, shard, shard, shard),
        check_vma=False,
    )
```

```python
import functools

import jax
import jax.numpy as jnp
from jax import lax
from jax.experimental import pallas as pl
from jax.experimental.pallas import tpu as pltpu
from jax.sharding import PartitionSpec as P

ADAM_STEP = 20
beta_one = 0.9
beta_two = 0.95
epsilon = 1e-08
decay_rate = 0.1
learn_rate = 0.001

MESH = pl.DeviceIdType.MESH
TOK, D, KV = 256, 8192, 512
HALF = KV // 2
PARTS = ((0, 96), (96, 96), (192, 64))
RS_ORDER = ((0, 1, 2), (1, 2, 0), (2, 0, 1))
AG_ORDER = ((2, 1, 0), (0, 2, 1), (1, 0, 2))
MOVE_ORDER = ((0, 1, 2), (1, 2, 0), (2, 0, 1))
XCHUNKS = 4


def device(x, y, z, core):
    return ((z // 4) * 2 + core, x * 16 + y * 4 + lax.rem(z, 4))


def coordinates():
    dp = lax.axis_index("dp")
    f = lax.axis_index("fsdp")
    core = lax.rem(dp, 2)
    return f // 16, lax.rem(f // 4, 4), (dp // 2) * 4 + lax.rem(f, 4), core


def kernel(
    x_hbm, cot_hbm, w_hbm, f_hbm, s_hbm, holder_ref,
    val_ref, gin_ref, gfull, new_a, new_b, new_c,
    cot_ref, w_ref, f_ref, s_ref, x_own, x_sib, cot_sib, cot_t, grad, gath, pair, order_ref, cot_sur, acc,
    in_0, in_1, in_2, next_0, next_1, next_2, last_in,
    mid_a, mid_b, mid_c, zsend, zrecv,
    loc_sem, pair_s, pair_r, xs_sem, xr_sem, ag_s, ag_r, ag2_s, ag2_r, sh_s, sh_r,
    rs0_s, rs0_r, rs_s, rs_r, mv_s, mv_r, ms_s, ms_r, fin_s, fin_r,
):
    x, y, z, core = coordinates()
    real = (x, y, z)
    size = (4, 4, 8)
    me = (x, y, lax.rem(z, 4))
    olds = (w_ref, f_ref, s_ref)
    mids = (mid_a, mid_b, mid_c)
    news = (new_a, new_b, new_c)
    first_in = (in_0, in_1, in_2)
    second_in = (next_0, next_1, next_2)

    def peer(axis, step):
        at = list(real)
        at[axis] = lax.rem(at[axis] + step + size[axis], size[axis])
        return device(*at, core)

    def slot(axis, step):
        return lax.rem(me[axis] + step + 4, 4)

    sibling = device(x, y, z, 1 - core)
    two = 2 - 4 * lax.rem(z, 2)
    sends = []

    def plan(src, dst, ssem, rsem, to):
        return pltpu.make_async_remote_copy(
            src_ref=src, dst_ref=dst, send_sem=ssem, recv_sem=rsem, device_id=to, device_id_type=MESH
        )

    def copy(src, dst, ssem, rsem, to):
        c = plan(src, dst, ssem, rsem, to)
        c.start()
        sends.append(c)
        return c

    small = []
    for i, (src, dst) in enumerate(((w_hbm, w_ref), (cot_hbm, cot_ref), (f_hbm, f_ref), (s_hbm, s_ref))):
        c = pltpu.make_async_copy(src, dst, loc_sem.at[XCHUNKS + i])
        c.start()
        small.append(c)
    width = D // XCHUNKS
    own = []
    spans = [lax.rem(x + step, 4) for step in (2, 1, 3, 0)]
    columns_of = [pl.ds(pl.multiple_of(span * width, width), width) for span in spans]
    for i in range(XCHUNKS):
        c = pltpu.make_async_copy(x_hbm.at[:, columns_of[i]], x_own.at[:, columns_of[i]], loc_sem.at[i])
        c.start()
        own.append(c)

    bar = pltpu.get_barrier_semaphore()
    greeted = [sibling, peer(2, 4)]
    greeted += [peer(a, d) for a in (0, 1) for d in (1, 2, -1)]
    greeted += [peer(2, d) for d in (1, -1, 2, -2)]
    for to in greeted:
        pl.semaphore_signal(bar, inc=1, device_id=to, device_id_type=MESH)

    small[0].wait()
    pl.semaphore_wait(bar, len(greeted))

    def ag_view(part, at, low, rows):
        if isinstance(at[2], slice):
            pairs, member = at[2], at[2]
        else:
            pairs, member = at[2] // 2, lax.rem(at[2], 2)
        return gath.at[at[0], at[1], pairs, member, pl.ds(core * HALF + PARTS[part][0] + low, rows), :]

    ag = {}

    def ag_send(part, stage):
        order = AG_ORDER[part]
        axis = order[stage]
        rows = PARTS[part][1]
        half = rows // 2
        at = list(me)
        for a in order[:stage]:
            at[a] = slice(None)
        for k, (step, low, n) in enumerate(((1, 0, rows), (-1, 0, rows), (2, 0, half), (-2, half, half))):
            view = ag_view(part, at, low, n)
            ag[part, stage, k] = copy(
                view, view, ag_s.at[part, stage, k], ag_r.at[part, stage, k], peer(axis, step)
            )

    def ag_finish(part, stage):
        for k in range(4):
            ag[part, stage, k].wait_recv()

    def ag2_at(part, value):
        at = [slice(None)] * 3
        at[AG_ORDER[part][2]] = value
        return at

    def ag2_send(part):
        axis = AG_ORDER[part][2]
        half = PARTS[part][1] // 2
        for first in (True, False):
            for k, step in enumerate((1, -1)):
                low = 0 if (k == 0) == first else half
                j = k if first else 4 + k
                view = ag_view(part, ag2_at(part, me[axis]), low, half)
                ag[part, 2, j] = copy(view, view, ag2_s.at[part, j], ag2_r.at[part, j], peer(axis, step))

    def ag2_forward(part):
        axis = AG_ORDER[part][2]
        half = PARTS[part][1] // 2
        for k, (step, low) in enumerate(((1, 0), (-1, half))):
            ag[part, 2, k].wait_recv()
            view = ag_view(part, ag2_at(part, slot(axis, -step)), low, half)
            ag[part, 2, 2 + k] = copy(view, view, ag2_s.at[part, 2 + k], ag2_r.at[part, 2 + k], peer(axis, step))

    def ag2_finish(part):
        for k in (2, 3, 4, 5):
            ag[part, 2, k].wait_recv()

    share = {}

    def ag_share(part):
        view = ag_view(part, (slice(None),) * 3, 0, PARTS[part][1])
        share[part] = copy(view, view, sh_s.at[part], sh_r.at[part], sibling)

    mv = {}
    active = [lax.rem(me[MOVE_ORDER[n][2]], 2) == core for n in range(3)]

    def mv_view(n, stage, value):
        axis = MOVE_ORDER[n][stage]
        if stage == 0:
            idx = [slice(None)] * 3
            idx[axis] = value
            return olds[n].at[idx[0], idx[1], idx[2]]
        if stage == 1:
            rest = [a for a in range(3) if a != MOVE_ORDER[n][0]]
            if rest[0] == axis:
                return mids[n].at[0, :, value]
            return mids[n].at[0, :, :, value]
        return mids[n].at[1, :, :, value]

    def mv_dst(n, stage, value):
        return news[n].at[value] if stage == 2 else mids[n].at[stage, value]

    def mv_send(n, stage):
        axis = MOVE_ORDER[n][stage]
        for k, step in enumerate((1, -1, 2)):
            far = two if (axis == 2 and step == 2) else step
            mv[n, stage, k] = plan(
                mv_view(n, stage, slot(axis, step)), mv_dst(n, stage, me[axis]),
                mv_s.at[n, stage, k], mv_r.at[n, stage, k], peer(axis, far),
            )
        home = mv_dst(n, stage, me[axis])
        here = mv_view(n, stage, me[axis])

        @pl.when(active[n])
        def _():
            for k in range(3):
                mv[n, stage, k].start()
            home[...] = here[...]

    def mv_finish(n, stage):
        @pl.when(active[n])
        def _():
            for k in range(3) if stage < 2 else (2,):
                mv[n, stage, k].wait_recv()

        if stage == 2:
            @pl.when(jnp.logical_not(active[n]))
            def _():
                mv[n, stage, 0].wait_recv()
                mv[n, stage, 1].wait_recv()

    def mv_share(n):
        for k in range(2):
            view = news[n].at[core + 2 * k]
            mv[n, 3, k] = copy(view, view, ms_s.at[n, k], ms_r.at[n, k], sibling)

    rs = {}

    def rs_view(part, stage, value, low, rows):
        order = RS_ORDER[part]
        at = [me[0], me[1], me[2]]
        at[order[stage]] = value
        for a in order[stage + 1:]:
            at[a] = slice(None)
        return grad.at[at[0], at[1], at[2], pl.ds(PARTS[part][0] + low, rows), :]

    def rs_buf(part, stage, which, low, rows):
        if stage == 0:
            return first_in[part].at[which, :, :, pl.ds(low, rows), :]
        if stage == 1:
            return second_in[part].at[which, :, pl.ds(low, rows), :]
        return last_in.at[which, pl.ds(PARTS[part][0] + low, rows), :]

    def rs0_copy(part, k, value, low, rows, which, step):
        axis = RS_ORDER[part][0]
        rs[part, 0, k] = copy(
            rs_view(part, 0, value, low, rows), rs_buf(part, 0, which, low, rows),
            rs0_s.at[part, k], rs0_r.at[part, k], peer(axis, step),
        )

    def rs0_far(part):
        axis = RS_ORDER[part][0]
        half = PARTS[part][1] // 2
        rs0_copy(part, 0, slot(axis, 2), 0, half, 2, 1)
        rs0_copy(part, 1, slot(axis, 2), half, half, 2, -1)

    def rs0_near(part):
        axis = RS_ORDER[part][0]
        half = PARTS[part][1] // 2
        rs0_copy(part, 2, slot(axis, 1), half, half, 0, 1)
        rs0_copy(part, 3, slot(axis, -1), 0, half, 1, -1)

    def add(view, *others):
        total = view[...].astype(jnp.float32)
        for o in others:
            total = total + o[...].astype(jnp.float32)
        return total.astype(jnp.bfloat16)

    def rs0_forward(part):
        axis = RS_ORDER[part][0]
        half = PARTS[part][1] // 2
        for k, (step, low) in enumerate(((1, 0), (-1, half))):
            value = slot(axis, step)
            rs[part, 0, k].wait_recv()
            for i in range(4):
                view = rs_view(part, 0, value, low, half).at[i]
                view[...] = add(view, rs_buf(part, 0, 2, low, half).at[i])
            rs0_copy(part, 4 + k, value, low, half, k, step)

    def rs_copy(part, stage, k, value, low, rows, which, step):
        axis = RS_ORDER[part][stage]
        rs[part, stage, k] = copy(
            rs_view(part, stage, value, low, rows), rs_buf(part, stage, which, low, rows),
            rs_s.at[part, stage - 1, k], rs_r.at[part, stage - 1, k], peer(axis, step),
        )

    def rs_send(part, stage):
        axis = RS_ORDER[part][stage]
        rows = PARTS[part][1]
        half = rows // 2
        rs_copy(part, stage, 0, slot(axis, 1), 0, rows, 0, 1)
        rs_copy(part, stage, 1, slot(axis, -1), 0, rows, 1, -1)
        rs_copy(part, stage, 2, slot(axis, 2), 0, half, 2, 2)
        rs_copy(part, stage, 3, slot(axis, 2), half, half, 2, -2)

    def rs0_finish(part):
        axis = RS_ORDER[part][0]
        rows = PARTS[part][1]
        for k in (2, 3, 4, 5):
            rs[part, 0, k].wait_recv()
        for i in range(4):
            view = rs_view(part, 0, me[axis], 0, rows).at[i]
            view[...] = add(view, *[rs_buf(part, 0, which, 0, rows).at[i] for which in range(2)])
        rs_send(part, 1)

    def rs_finish(part, stage):
        rows = PARTS[part][1]
        for k in range(4):
            rs[part, stage, k].wait_recv()
        view = rs_view(part, stage, me[RS_ORDER[part][stage]], 0, rows)
        total = add(view, *[rs_buf(part, stage, which, 0, rows) for which in range(3)])
        if stage == 1:
            view[...] = total
            rs_send(part, 2)
        else:
            lines = pl.ds(PARTS[part][0], rows)
            zsend[lines, :] = total
            rs[part, 3] = copy(
                zsend.at[lines, :], zrecv.at[lines, :], fin_s.at[part], fin_r.at[part], peer(2, 4)
            )

    def grad_chunk(i, carry):
        at = pl.ds(pl.multiple_of(i * 512, 512), 512)
        total = jnp.dot(cot_t[:, pl.ds(0, TOK)], x_own[:, at], preferred_element_type=jnp.float32)
        total = total + jnp.dot(cot_t[:, pl.ds(TOK, TOK)], x_sib[:, at], preferred_element_type=jnp.float32)
        total = (total * (1.0 / 256.0)).astype(jnp.bfloat16)
        for k in range(4):
            grad[i // 4, lax.rem(i, 4), k] = total[:, k * 128:(k + 1) * 128]
        return carry

    def project(t, carry):
        rows = pl.ds(pl.multiple_of((t // 8) * HALF + lax.rem(t, 4) * 64, 64), 64)
        tiles = gath[:, :, :, lax.rem(t // 4, 2), rows, :]
        columns = jnp.concatenate(
            [tiles[:, :, :, 16 * j:16 * j + 16, :].reshape(KV, 128) for j in range(4)], axis=1
        )
        at = pl.ds(pl.multiple_of(t * 512, 512), 512)
        acc[...] += lax.dot_general(
            x_own[:, at], columns, (((1,), (1,)), ((), ())), preferred_element_type=jnp.float32
        )
        gin_ref[:, at] = jnp.dot(cot_sur[...], columns, preferred_element_type=jnp.float32).astype(
            jnp.bfloat16
        )
        return carry

    parity = lax.rem(z, 2)
    pair_copy = copy(
        w_ref.at[2 * core + 1 - parity], pair, pair_s.at[0], pair_r.at[0], peer(2, 1 - 2 * parity)
    )
    for c in small[1:]:
        c.wait()
    cot_copy = copy(
        cot_ref.at[:, pl.ds(pl.multiple_of((1 - core) * HALF, HALF), HALF)], cot_sib,
        xs_sem.at[XCHUNKS], xr_sem.at[XCHUNKS], sibling,
    )
    for n in range(3):
        mv_send(n, 0)
    xcopy = []
    for i in range(XCHUNKS):
        xcopy.append(
            copy(
                x_hbm.at[:, columns_of[i]], x_sib.at[:, columns_of[i]],
                xs_sem.at[i], xr_sem.at[i], sibling,
            )
        )
    mine = w_ref[2 * core + parity].reshape(16, 8, 128)
    pair_copy.wait_recv()
    other = pair[...].reshape(16, 8, 128)
    both = jnp.concatenate(
        [jnp.where(parity == 0, mine, other), jnp.where(parity == 0, other, mine)], axis=1
    )
    gath[me[0], me[1], me[2] // 2, parity, pl.ds(core * HALF, HALF), :] = both.reshape(HALF, 128).astype(
        jnp.bfloat16
    )
    for part in range(3):
        ag_send(part, 0)

    def grad_span(i):
        own[i].wait()
        xcopy[i].wait_recv()
        lax.fori_loop(4 * spans[i], 4 * spans[i] + 4, grad_chunk, 0)

    cot_copy.wait_recv()
    cot_half = cot_ref[:, pl.ds(pl.multiple_of(core * HALF, HALF), HALF)]
    cot_t[:, pl.ds(0, TOK)] = cot_half.astype(jnp.float32).T.astype(jnp.bfloat16)
    cot_t[:, pl.ds(TOK, TOK)] = cot_sib[...].astype(jnp.float32).T.astype(jnp.bfloat16)
    grad_span(0)
    rs0_far(0)
    for part in range(3):
        ag_finish(part, 0)
        ag_send(part, 1)
    grad_span(1)
    grad_span(2)
    rs0_near(0)
    grad_span(3)
    for part in (1, 2):
        rs0_far(part)
    for part in (1, 2):
        rs0_near(part)
    for n in range(3):
        mv_finish(n, 0)
        mv_send(n, 1)
    for part in range(3):
        ag_finish(part, 1)
        ag2_send(part)
    rs0_forward(0)
    lane_block = lax.broadcasted_iota(jnp.int32, (1, KV), 1) // 8
    target = lax.rem(lax.broadcasted_iota(jnp.int32, (1, KV), 1), 8)
    for p in range(64):
        target = jnp.where(lane_block == p, target + 8 * holder_ref[p], target)
    hit = lax.broadcasted_iota(jnp.int32, (KV, KV), 0) == target
    order_ref[...] = jnp.where(hit, 1.0, 0.0).astype(jnp.bfloat16)
    cot_sur[...] = jnp.dot(cot_ref[...], order_ref[...], preferred_element_type=jnp.float32).astype(jnp.bfloat16)
    acc[...] = jnp.zeros_like(acc)
    for part in (1, 2):
        rs0_forward(part)
    for n in range(3):
        mv_finish(n, 1)
        mv_send(n, 2)
    for part in range(3):
        ag2_forward(part)
    for part in range(3):
        rs0_finish(part)
    for part in range(3):
        ag2_finish(part)
        ag_share(part)
    for n in range(3):
        mv_finish(n, 2)
        mv_share(n)
    for part in range(3):
        rs_finish(part, 1)
    for part in range(3):
        share[part].wait_recv()
    lax.fori_loop(0, 8, project, 0)
    for part in range(3):
        rs_finish(part, 2)
    lax.fori_loop(8, 16, project, 0)
    val_ref[...] = lax.dot_general(
        acc[...].astype(jnp.bfloat16), order_ref[...], (((1,), (1,)), ((), ())),
        preferred_element_type=jnp.float32,
    ).astype(jnp.bfloat16)
    for n in range(3):
        mv[n, 3, 0].wait_recv()
        mv[n, 3, 1].wait_recv()
    for part in range(3):
        rs[part, 3].wait_recv()
    half_rows = pl.ds(pl.multiple_of(core * HALF, HALF), HALF)
    gfull[half_rows, :] = zsend[...].astype(jnp.float32) + zrecv[...].astype(jnp.float32)
    last = copy(gfull.at[half_rows, :], gfull.at[half_rows, :], fin_s.at[3], fin_r.at[3], sibling)
    last.wait_recv()
    for n in range(3):
        @pl.when(active[n])
        def _(n=n):
            for stage in range(3):
                for k in range(3):
                    mv[n, stage, k].wait_send()
    for c in sends:
        c.wait_send()


def update_kernel(
    holder_ref, val_ref, gin_ref, grad_ref, w_ref, f_ref, s_ref, val_out, gin_out, nw_ref, nf_ref, ns_ref, weight_ref, first_ref, second_ref, sem
):
    copies = [
        pltpu.make_async_copy(gin_ref, gin_out, sem.at[0]),
        pltpu.make_async_copy(val_ref, val_out, sem.at[1]),
    ]
    for c in copies:
        c.start()

    targets = (weight_ref, first_ref, second_ref)
    for p in range(64):
        at = (p // 16, (p // 4) % 4, p % 4)
        rows = pl.ds(pl.multiple_of(holder_ref[p] * 8, 8), 8)
        for ref, order, out in zip((w_ref, f_ref, s_ref), MOVE_ORDER, targets):
            out[rows, :] = ref[at[order[2]], at[order[1]], at[order[0]]]
    gradient = grad_ref[...]
    weight = weight_ref[...]
    first_new = beta_one * first_ref[...] + (1.0 - beta_one) * gradient
    second_new = beta_two * second_ref[...] + (1.0 - beta_two) * gradient * gradient
    corrected = (
        first_new
        / (1.0 - beta_one**ADAM_STEP)
        / (jnp.sqrt(second_new / (1.0 - beta_two**ADAM_STEP)) + epsilon)
    )
    nw_ref[...] = (weight - learn_rate * (corrected + decay_rate * weight)).T
    nf_ref[...] = first_new.T
    ns_ref[...] = second_new.T
    for c in copies:
        c.wait()


def on_device(inputs, cotangent, old_weight, old_first, old_second, holder):
    def tiles(a):
        return a.reshape(8, 64, 128).transpose(1, 0, 2).reshape(4, 4, 4, 8, 128)

    bf, f32 = jnp.bfloat16, jnp.float32
    vmem = pl.BlockSpec(memory_space=pltpu.VMEM)
    smem = pl.BlockSpec(memory_space=pltpu.SMEM)
    anywhere = pl.BlockSpec(memory_space=pl.ANY)
    hbm = pl.BlockSpec(memory_space=pltpu.HBM)
    dma = pltpu.SemaphoreType.DMA
    state = (4, 4, 4, 8, 128)
    parts = pl.pallas_call(
        kernel,
        out_shape=(
            pltpu.VMEM((TOK, KV), bf),
            pltpu.VMEM((TOK, D), bf),
            pltpu.VMEM((KV, 128), f32),
            pltpu.VMEM(state, f32),
            pltpu.VMEM(state, f32),
            pltpu.VMEM(state, f32),
        ),
        in_specs=[hbm] * 5 + [smem],
        out_specs=(vmem,) * 6,
        scratch_shapes=[
            pltpu.VMEM((TOK, KV), bf),
            *[pltpu.VMEM(state, f32)] * 3,
            pltpu.VMEM((TOK, D), bf),
            pltpu.VMEM((TOK, D), bf),
            pltpu.VMEM((TOK, HALF), bf),
            pltpu.VMEM((HALF, 2 * TOK), bf),
            pltpu.VMEM((4, 4, 4, HALF, 128), bf),
            pltpu.VMEM((4, 4, 2, 2, KV, 128), bf),
            pltpu.VMEM((4, 4, 8, 128), f32),
            pltpu.VMEM((KV, KV), bf),
            pltpu.VMEM((TOK, KV), bf),
            pltpu.VMEM((TOK, KV), f32),
            *[pltpu.VMEM((3, 4, 4, rows, 128), bf) for _, rows in PARTS],
            *[pltpu.VMEM((3, 4, rows, 128), bf) for _, rows in PARTS],
            pltpu.VMEM((3, HALF, 128), bf),
            *[pltpu.VMEM((2,) + (4, 4, 4, 8, 128), f32)] * 3,
            pltpu.VMEM((HALF, 128), bf),
            pltpu.VMEM((HALF, 128), bf),
            dma((XCHUNKS + 4,)),
            dma((1,)),
            dma((1,)),
            dma((XCHUNKS + 1,)),
            dma((XCHUNKS + 1,)),
            dma((3, 2, 4)),
            dma((3, 2, 4)),
            dma((3, 6)),
            dma((3, 6)),
            dma((3,)),
            dma((3,)),
            dma((3, 6)),
            dma((3, 6)),
            dma((3, 2, 4)),
            dma((3, 2, 4)),
            dma((3, 3, 3)),
            dma((3, 3, 3)),
            dma((3, 2)),
            dma((3, 2)),
            dma((4,)),
            dma((4,)),
        ],
        compiler_params=pltpu.CompilerParams(
            collective_id=0, has_side_effects=True, vmem_limit_bytes=117 * 2**19
        ),
    )(inputs, cotangent, tiles(old_weight), tiles(old_first), tiles(old_second), holder)
    values, grad_input, gradient, weight, first, second = parts
    shard = jax.ShapeDtypeStruct((128, KV), f32)
    return pl.pallas_call(
        update_kernel,
        out_shape=(
            jax.ShapeDtypeStruct((TOK, KV), bf),
            jax.ShapeDtypeStruct((TOK, D), bf),
            shard,
            shard,
            shard,
        ),
        in_specs=[smem] + [vmem] * 6,
        out_specs=(anywhere, anywhere, vmem, vmem, vmem),
        scratch_shapes=[pltpu.VMEM((KV, 128), f32)] * 3 + [dma((2,))],
        compiler_params=pltpu.CompilerParams(vmem_limit_bytes=16 * 2**20),
    )(holder, values, grad_input, gradient, weight, first, second)


def solution(mesh):
    rows = P(("dp", "fsdp"), None)
    shard = P("fsdp", None)
    return jax.shard_map(
        on_device,
        mesh=mesh,
        in_specs=(rows, rows, shard, shard, shard, P()),
        out_specs=(rows, rows, shard, shard, shard),
        check_vma=False,
    )
```

```python
import functools

import jax
import jax.numpy as jnp
from jax import lax
from jax.experimental import pallas as pl
from jax.experimental.pallas import tpu as pltpu
from jax.sharding import PartitionSpec as P

ADAM_STEP = 20
beta_one = 0.9
beta_two = 0.95
epsilon = 1e-08
decay_rate = 0.1
learn_rate = 0.001

MESH = pl.DeviceIdType.MESH
TOK, D, KV = 256, 8192, 512
HALF = KV // 2
PARTS = ((0, 96), (96, 96), (192, 64))
RS_ORDER = ((0, 1, 2), (1, 2, 0), (2, 0, 1))
AG_ORDER = ((2, 1, 0), (0, 2, 1), (1, 0, 2))
MOVE_ORDER = ((0, 1, 2), (1, 2, 0), (2, 0, 1))
XCHUNKS = 4


def device(x, y, z, core):
    return ((z // 4) * 2 + core, x * 16 + y * 4 + lax.rem(z, 4))


def coordinates():
    dp = lax.axis_index("dp")
    f = lax.axis_index("fsdp")
    core = lax.rem(dp, 2)
    return f // 16, lax.rem(f // 4, 4), (dp // 2) * 4 + lax.rem(f, 4), core


def kernel(
    x_hbm, cot_hbm, w_hbm, f_hbm, s_hbm, holder_ref,
    val_ref, gin_ref, gfull, new_a, new_b, new_c,
    cot_ref, w_ref, f_ref, s_ref, x_own, x_sib, cot_sib, cot_t, grad, gath, pair, order_ref, cot_sur, acc,
    in_0, in_1, in_2, next_0, next_1, next_2, last_in,
    mid_a, mid_b, mid_c, zsend, zrecv,
    loc_sem, pair_s, pair_r, xs_sem, xr_sem, ag_s, ag_r, ag2_s, ag2_r, sh_s, sh_r,
    rs0_s, rs0_r, rs_s, rs_r, mv_s, mv_r, ms_s, ms_r, fin_s, fin_r,
):
    x, y, z, core = coordinates()
    real = (x, y, z)
    size = (4, 4, 8)
    me = (x, y, lax.rem(z, 4))
    olds = (w_ref, f_ref, s_ref)
    mids = (mid_a, mid_b, mid_c)
    news = (new_a, new_b, new_c)
    first_in = (in_0, in_1, in_2)
    second_in = (next_0, next_1, next_2)

    def peer(axis, step):
        at = list(real)
        at[axis] = lax.rem(at[axis] + step + size[axis], size[axis])
        return device(*at, core)

    def slot(axis, step):
        return lax.rem(me[axis] + step + 4, 4)

    sibling = device(x, y, z, 1 - core)
    two = 2 - 4 * lax.rem(z, 2)
    sends = []

    def plan(src, dst, ssem, rsem, to):
        return pltpu.make_async_remote_copy(
            src_ref=src, dst_ref=dst, send_sem=ssem, recv_sem=rsem, device_id=to, device_id_type=MESH
        )

    def copy(src, dst, ssem, rsem, to):
        c = plan(src, dst, ssem, rsem, to)
        c.start()
        sends.append(c)
        return c

    small = []
    for i, (src, dst) in enumerate(((w_hbm, w_ref), (cot_hbm, cot_ref), (f_hbm, f_ref), (s_hbm, s_ref))):
        c = pltpu.make_async_copy(src, dst, loc_sem.at[XCHUNKS + i])
        c.start()
        small.append(c)
    width = D // XCHUNKS
    own = []
    spans = [lax.rem(x + step, 4) for step in (2, 1, 3, 0)]
    columns_of = [pl.ds(pl.multiple_of(span * width, width), width) for span in spans]
    for i in range(XCHUNKS):
        c = pltpu.make_async_copy(x_hbm.at[:, columns_of[i]], x_own.at[:, columns_of[i]], loc_sem.at[i])
        c.start()
        own.append(c)

    bar = pltpu.get_barrier_semaphore()
    greeted = [sibling, peer(2, 4)]
    greeted += [peer(a, d) for a in (0, 1) for d in (1, 2, -1)]
    greeted += [peer(2, d) for d in (1, -1, 2, -2)]
    for to in greeted:
        pl.semaphore_signal(bar, inc=1, device_id=to, device_id_type=MESH)

    small[0].wait()
    pl.semaphore_wait(bar, len(greeted))

    def ag_view(part, at, low, rows):
        if isinstance(at[2], slice):
            pairs, member = at[2], at[2]
        else:
            pairs, member = at[2] // 2, lax.rem(at[2], 2)
        return gath.at[at[0], at[1], pairs, member, pl.ds(core * HALF + PARTS[part][0] + low, rows), :]

    ag = {}

    def ag_send(part, stage):
        order = AG_ORDER[part]
        axis = order[stage]
        rows = PARTS[part][1]
        half = rows // 2
        at = list(me)
        for a in order[:stage]:
            at[a] = slice(None)
        for k, (step, low, n) in enumerate(((1, 0, rows), (-1, 0, rows), (2, 0, half), (-2, half, half))):
            view = ag_view(part, at, low, n)
            ag[part, stage, k] = copy(
                view, view, ag_s.at[part, stage, k], ag_r.at[part, stage, k], peer(axis, step)
            )

    def ag_finish(part, stage):
        for k in range(4):
            ag[part, stage, k].wait_recv()

    def ag2_at(part, value):
        at = [slice(None)] * 3
        at[AG_ORDER[part][2]] = value
        return at

    def ag2_send(part):
        axis = AG_ORDER[part][2]
        half = PARTS[part][1] // 2
        for first in (True, False):
            for k, step in enumerate((1, -1)):
                low = 0 if (k == 0) == first else half
                j = k if first else 4 + k
                view = ag_view(part, ag2_at(part, me[axis]), low, half)
                ag[part, 2, j] = copy(view, view, ag2_s.at[part, j], ag2_r.at[part, j], peer(axis, step))

    def ag2_forward(part):
        axis = AG_ORDER[part][2]
        half = PARTS[part][1] // 2
        for k, (step, low) in enumerate(((1, 0), (-1, half))):
            ag[part, 2, k].wait_recv()
            view = ag_view(part, ag2_at(part, slot(axis, -step)), low, half)
            ag[part, 2, 2 + k] = copy(view, view, ag2_s.at[part, 2 + k], ag2_r.at[part, 2 + k], peer(axis, step))

    def ag2_finish(part):
        for k in (2, 3, 4, 5):
            ag[part, 2, k].wait_recv()

    share = {}

    def ag_share(part):
        view = ag_view(part, (slice(None),) * 3, 0, PARTS[part][1])
        share[part] = copy(view, view, sh_s.at[part], sh_r.at[part], sibling)

    mv = {}
    active = [lax.rem(me[MOVE_ORDER[n][2]], 2) == core for n in range(3)]

    def mv_view(n, stage, value):
        axis = MOVE_ORDER[n][stage]
        if stage == 0:
            idx = [slice(None)] * 3
            idx[axis] = value
            return olds[n].at[idx[0], idx[1], idx[2]]
        if stage == 1:
            rest = [a for a in range(3) if a != MOVE_ORDER[n][0]]
            if rest[0] == axis:
                return mids[n].at[0, :, value]
            return mids[n].at[0, :, :, value]
        return mids[n].at[1, :, :, value]

    def mv_dst(n, stage, value):
        return news[n].at[value] if stage == 2 else mids[n].at[stage, value]

    def mv_send(n, stage):
        axis = MOVE_ORDER[n][stage]
        for k, step in enumerate((1, -1, 2)):
            far = two if (axis == 2 and step == 2) else step
            mv[n, stage, k] = plan(
                mv_view(n, stage, slot(axis, step)), mv_dst(n, stage, me[axis]),
                mv_s.at[n, stage, k], mv_r.at[n, stage, k], peer(axis, far),
            )
        home = mv_dst(n, stage, me[axis])
        here = mv_view(n, stage, me[axis])

        @pl.when(active[n])
        def _():
            for k in range(3):
                mv[n, stage, k].start()
            home[...] = here[...]

    def mv_finish(n, stage):
        @pl.when(active[n])
        def _():
            for k in range(3) if stage < 2 else (2,):
                mv[n, stage, k].wait_recv()

        if stage == 2:
            @pl.when(jnp.logical_not(active[n]))
            def _():
                mv[n, stage, 0].wait_recv()
                mv[n, stage, 1].wait_recv()

    def mv_share(n):
        for k in range(2):
            view = news[n].at[core + 2 * k]
            mv[n, 3, k] = copy(view, view, ms_s.at[n, k], ms_r.at[n, k], sibling)

    rs = {}

    def rs_view(part, stage, value, low, rows):
        order = RS_ORDER[part]
        at = [me[0], me[1], me[2]]
        at[order[stage]] = value
        for a in order[stage + 1:]:
            at[a] = slice(None)
        return grad.at[at[0], at[1], at[2], pl.ds(PARTS[part][0] + low, rows), :]

    def rs_buf(part, stage, which, low, rows):
        if stage == 0:
            return first_in[part].at[which, :, :, pl.ds(low, rows), :]
        if stage == 1:
            return second_in[part].at[which, :, pl.ds(low, rows), :]
        return last_in.at[which, pl.ds(PARTS[part][0] + low, rows), :]

    def rs0_copy(part, k, value, low, rows, which, step):
        axis = RS_ORDER[part][0]
        rs[part, 0, k] = copy(
            rs_view(part, 0, value, low, rows), rs_buf(part, 0, which, low, rows),
            rs0_s.at[part, k], rs0_r.at[part, k], peer(axis, step),
        )

    def rs0_far(part):
        axis = RS_ORDER[part][0]
        half = PARTS[part][1] // 2
        rs0_copy(part, 0, slot(axis, 2), 0, half, 2, 1)
        rs0_copy(part, 1, slot(axis, 2), half, half, 2, -1)

    def rs0_near(part):
        axis = RS_ORDER[part][0]
        half = PARTS[part][1] // 2
        rs0_copy(part, 2, slot(axis, 1), half, half, 0, 1)
        rs0_copy(part, 3, slot(axis, -1), 0, half, 1, -1)

    def add(view, *others):
        total = view[...].astype(jnp.float32)
        for o in others:
            total = total + o[...].astype(jnp.float32)
        return total.astype(jnp.bfloat16)

    def rs0_forward(part):
        axis = RS_ORDER[part][0]
        half = PARTS[part][1] // 2
        for k, (step, low) in enumerate(((1, 0), (-1, half))):
            value = slot(axis, step)
            rs[part, 0, k].wait_recv()
            for i in range(4):
                view = rs_view(part, 0, value, low, half).at[i]
                view[...] = add(view, rs_buf(part, 0, 2, low, half).at[i])
            rs0_copy(part, 4 + k, value, low, half, k, step)

    def rs_copy(part, stage, k, value, low, rows, which, step):
        axis = RS_ORDER[part][stage]
        rs[part, stage, k] = copy(
            rs_view(part, stage, value, low, rows), rs_buf(part, stage, which, low, rows),
            rs_s.at[part, stage - 1, k], rs_r.at[part, stage - 1, k], peer(axis, step),
        )

    def rs_send(part, stage):
        axis = RS_ORDER[part][stage]
        rows = PARTS[part][1]
        half = rows // 2
        rs_copy(part, stage, 0, slot(axis, 1), 0, rows, 0, 1)
        rs_copy(part, stage, 1, slot(axis, -1), 0, rows, 1, -1)
        rs_copy(part, stage, 2, slot(axis, 2), 0, half, 2, 2)
        rs_copy(part, stage, 3, slot(axis, 2), half, half, 2, -2)

    def rs0_finish(part):
        axis = RS_ORDER[part][0]
        rows = PARTS[part][1]
        for k in (2, 3, 4, 5):
            rs[part, 0, k].wait_recv()
        for i in range(4):
            view = rs_view(part, 0, me[axis], 0, rows).at[i]
            view[...] = add(view, *[rs_buf(part, 0, which, 0, rows).at[i] for which in range(2)])
        rs_send(part, 1)

    def rs_finish(part, stage):
        rows = PARTS[part][1]
        for k in range(4):
            rs[part, stage, k].wait_recv()
        view = rs_view(part, stage, me[RS_ORDER[part][stage]], 0, rows)
        total = add(view, *[rs_buf(part, stage, which, 0, rows) for which in range(3)])
        if stage == 1:
            view[...] = total
            rs_send(part, 2)
        else:
            lines = pl.ds(PARTS[part][0], rows)
            zsend[lines, :] = total
            rs[part, 3] = copy(
                zsend.at[lines, :], zrecv.at[lines, :], fin_s.at[part], fin_r.at[part], peer(2, 4)
            )

    def grad_chunk(i, carry):
        at = pl.ds(pl.multiple_of(i * 512, 512), 512)
        total = jnp.dot(cot_t[:, pl.ds(0, TOK)], x_own[:, at], preferred_element_type=jnp.float32)
        total = total + jnp.dot(cot_t[:, pl.ds(TOK, TOK)], x_sib[:, at], preferred_element_type=jnp.float32)
        total = (total * (1.0 / 256.0)).astype(jnp.bfloat16)
        for k in range(4):
            grad[i // 4, lax.rem(i, 4), k] = total[:, k * 128:(k + 1) * 128]
        return carry

    def project(t, carry):
        rows = pl.ds(pl.multiple_of((t // 8) * HALF + lax.rem(t, 4) * 64, 64), 64)
        tiles = gath[:, :, :, lax.rem(t // 4, 2), rows, :]
        columns = jnp.concatenate(
            [tiles[:, :, :, 16 * j:16 * j + 16, :].reshape(KV, 128) for j in range(4)], axis=1
        )
        at = pl.ds(pl.multiple_of(t * 512, 512), 512)
        acc[...] += lax.dot_general(
            x_own[:, at], columns, (((1,), (1,)), ((), ())), preferred_element_type=jnp.float32
        )
        gin_ref[:, at] = jnp.dot(cot_sur[...], columns, preferred_element_type=jnp.float32).astype(
            jnp.bfloat16
        )
        return carry

    parity = lax.rem(z, 2)
    pair_copy = copy(
        w_ref.at[2 * core + 1 - parity], pair, pair_s.at[0], pair_r.at[0], peer(2, 1 - 2 * parity)
    )
    for c in small[1:]:
        c.wait()
    cot_copy = copy(
        cot_ref.at[:, pl.ds(pl.multiple_of((1 - core) * HALF, HALF), HALF)], cot_sib,
        xs_sem.at[XCHUNKS], xr_sem.at[XCHUNKS], sibling,
    )
    for n in range(3):
        mv_send(n, 0)
    xcopy = []
    for i in range(XCHUNKS):
        xcopy.append(
            copy(
                x_hbm.at[:, columns_of[i]], x_sib.at[:, columns_of[i]],
                xs_sem.at[i], xr_sem.at[i], sibling,
            )
        )
    mine = w_ref[2 * core + parity].reshape(16, 8, 128)
    pair_copy.wait_recv()
    other = pair[...].reshape(16, 8, 128)
    both = jnp.concatenate(
        [jnp.where(parity == 0, mine, other), jnp.where(parity == 0, other, mine)], axis=1
    )
    gath[me[0], me[1], me[2] // 2, parity, pl.ds(core * HALF, HALF), :] = both.reshape(HALF, 128).astype(
        jnp.bfloat16
    )
    for part in range(3):
        ag_send(part, 0)

    def grad_span(i):
        own[i].wait()
        xcopy[i].wait_recv()
        lax.fori_loop(4 * spans[i], 4 * spans[i] + 4, grad_chunk, 0)

    cot_copy.wait_recv()
    cot_half = cot_ref[:, pl.ds(pl.multiple_of(core * HALF, HALF), HALF)]
    cot_t[:, pl.ds(0, TOK)] = cot_half.astype(jnp.float32).T.astype(jnp.bfloat16)
    cot_t[:, pl.ds(TOK, TOK)] = cot_sib[...].astype(jnp.float32).T.astype(jnp.bfloat16)
    grad_span(0)
    rs0_far(0)
    for part in range(3):
        ag_finish(part, 0)
        ag_send(part, 1)
    grad_span(1)
    grad_span(2)
    rs0_near(0)
    grad_span(3)
    for part in (1, 2):
        rs0_far(part)
    for part in (1, 2):
        rs0_near(part)
    for part in range(3):
        ag_finish(part, 1)
        ag2_send(part)
    rs0_forward(0)
    lane_block = lax.broadcasted_iota(jnp.int32, (1, KV), 1) // 8
    target = lax.rem(lax.broadcasted_iota(jnp.int32, (1, KV), 1), 8)
    for p in range(64):
        target = jnp.where(lane_block == p, target + 8 * holder_ref[p], target)
    hit = lax.broadcasted_iota(jnp.int32, (KV, KV), 0) == target
    order_ref[...] = jnp.where(hit, 1.0, 0.0).astype(jnp.bfloat16)
    cot_sur[...] = jnp.dot(cot_ref[...], order_ref[...], preferred_element_type=jnp.float32).astype(jnp.bfloat16)
    acc[...] = jnp.zeros_like(acc)
    for part in (1, 2):
        rs0_forward(part)
    for part in range(3):
        ag2_forward(part)
    for part in range(3):
        rs0_finish(part)
    for n in range(3):
        mv_finish(n, 0)
        mv_send(n, 1)
    for part in range(3):
        ag2_finish(part)
        ag_share(part)
    for part in range(3):
        rs_finish(part, 1)
    for part in range(3):
        share[part].wait_recv()
    for n in range(3):
        mv_finish(n, 1)
        mv_send(n, 2)
    lax.fori_loop(0, 8, project, 0)
    for part in range(3):
        rs_finish(part, 2)
    lax.fori_loop(8, 16, project, 0)
    for n in range(3):
        mv_finish(n, 2)
        mv_share(n)
    val_ref[...] = lax.dot_general(
        acc[...].astype(jnp.bfloat16), order_ref[...], (((1,), (1,)), ((), ())),
        preferred_element_type=jnp.float32,
    ).astype(jnp.bfloat16)
    for n in range(3):
        mv[n, 3, 0].wait_recv()
        mv[n, 3, 1].wait_recv()
    for part in range(3):
        rs[part, 3].wait_recv()
    half_rows = pl.ds(pl.multiple_of(core * HALF, HALF), HALF)
    gfull[half_rows, :] = zsend[...].astype(jnp.float32) + zrecv[...].astype(jnp.float32)
    last = copy(gfull.at[half_rows, :], gfull.at[half_rows, :], fin_s.at[3], fin_r.at[3], sibling)
    last.wait_recv()
    for n in range(3):
        @pl.when(active[n])
        def _(n=n):
            for stage in range(3):
                for k in range(3):
                    mv[n, stage, k].wait_send()
    for c in sends:
        c.wait_send()


def update_kernel(
    holder_ref, val_ref, gin_ref, grad_ref, w_ref, f_ref, s_ref, val_out, gin_out, nw_ref, nf_ref, ns_ref, weight_ref, first_ref, second_ref,
    nw_out, nf_out, ns_out, sem
):
    copies = [
        pltpu.make_async_copy(gin_ref, gin_out, sem.at[0]),
        pltpu.make_async_copy(val_ref, val_out, sem.at[1]),
    ]
    for c in copies:
        c.start()

    targets = (weight_ref, first_ref, second_ref)
    for p in range(64):
        at = (p // 16, (p // 4) % 4, p % 4)
        rows = pl.ds(pl.multiple_of(holder_ref[p] * 8, 8), 8)
        for ref, order, out in zip((w_ref, f_ref, s_ref), MOVE_ORDER, targets):
            out[rows, :] = ref[at[order[2]], at[order[1]], at[order[0]]]
    def leave(i, value, staged, out):
        staged[...] = value.T
        c = pltpu.make_async_copy(staged, out, sem.at[i])
        c.start()
        copies.append(c)

    gradient = grad_ref[...]
    first_new = beta_one * first_ref[...] + (1.0 - beta_one) * gradient
    leave(2, first_new, nf_out, nf_ref)
    second_new = beta_two * second_ref[...] + (1.0 - beta_two) * gradient * gradient
    leave(3, second_new, ns_out, ns_ref)
    weight = weight_ref[...]
    corrected = (
        first_new
        / (1.0 - beta_one**ADAM_STEP)
        / (jnp.sqrt(second_new / (1.0 - beta_two**ADAM_STEP)) + epsilon)
    )
    leave(4, weight - learn_rate * (corrected + decay_rate * weight), nw_out, nw_ref)
    for c in copies:
        c.wait()


def on_device(inputs, cotangent, old_weight, old_first, old_second, holder):
    def tiles(a):
        return a.reshape(8, 64, 128).transpose(1, 0, 2).reshape(4, 4, 4, 8, 128)

    bf, f32 = jnp.bfloat16, jnp.float32
    vmem = pl.BlockSpec(memory_space=pltpu.VMEM)
    smem = pl.BlockSpec(memory_space=pltpu.SMEM)
    anywhere = pl.BlockSpec(memory_space=pl.ANY)
    hbm = pl.BlockSpec(memory_space=pltpu.HBM)
    dma = pltpu.SemaphoreType.DMA
    state = (4, 4, 4, 8, 128)
    parts = pl.pallas_call(
        kernel,
        out_shape=(
            pltpu.VMEM((TOK, KV), bf),
            pltpu.VMEM((TOK, D), bf),
            pltpu.VMEM((KV, 128), f32),
            pltpu.VMEM(state, f32),
            pltpu.VMEM(state, f32),
            pltpu.VMEM(state, f32),
        ),
        in_specs=[hbm] * 5 + [smem],
        out_specs=(vmem,) * 6,
        scratch_shapes=[
            pltpu.VMEM((TOK, KV), bf),
            *[pltpu.VMEM(state, f32)] * 3,
            pltpu.VMEM((TOK, D), bf),
            pltpu.VMEM((TOK, D), bf),
            pltpu.VMEM((TOK, HALF), bf),
            pltpu.VMEM((HALF, 2 * TOK), bf),
            pltpu.VMEM((4, 4, 4, HALF, 128), bf),
            pltpu.VMEM((4, 4, 2, 2, KV, 128), bf),
            pltpu.VMEM((4, 4, 8, 128), f32),
            pltpu.VMEM((KV, KV), bf),
            pltpu.VMEM((TOK, KV), bf),
            pltpu.VMEM((TOK, KV), f32),
            *[pltpu.VMEM((3, 4, 4, rows, 128), bf) for _, rows in PARTS],
            *[pltpu.VMEM((3, 4, rows, 128), bf) for _, rows in PARTS],
            pltpu.VMEM((3, HALF, 128), bf),
            *[pltpu.VMEM((2,) + (4, 4, 4, 8, 128), f32)] * 3,
            pltpu.VMEM((HALF, 128), bf),
            pltpu.VMEM((HALF, 128), bf),
            dma((XCHUNKS + 4,)),
            dma((1,)),
            dma((1,)),
            dma((XCHUNKS + 1,)),
            dma((XCHUNKS + 1,)),
            dma((3, 2, 4)),
            dma((3, 2, 4)),
            dma((3, 6)),
            dma((3, 6)),
            dma((3,)),
            dma((3,)),
            dma((3, 6)),
            dma((3, 6)),
            dma((3, 2, 4)),
            dma((3, 2, 4)),
            dma((3, 3, 3)),
            dma((3, 3, 3)),
            dma((3, 2)),
            dma((3, 2)),
            dma((4,)),
            dma((4,)),
        ],
        compiler_params=pltpu.CompilerParams(
            collective_id=0, has_side_effects=True, vmem_limit_bytes=117 * 2**19
        ),
    )(inputs, cotangent, tiles(old_weight), tiles(old_first), tiles(old_second), holder)
    values, grad_input, gradient, weight, first, second = parts
    shard = jax.ShapeDtypeStruct((128, KV), f32)
    return pl.pallas_call(
        update_kernel,
        out_shape=(
            jax.ShapeDtypeStruct((TOK, KV), bf),
            jax.ShapeDtypeStruct((TOK, D), bf),
            shard,
            shard,
            shard,
        ),
        in_specs=[smem] + [vmem] * 6,
        out_specs=(anywhere,) * 5,
        scratch_shapes=[pltpu.VMEM((KV, 128), f32)] * 3 + [pltpu.VMEM((128, KV), f32)] * 3 + [dma((5,))],
        compiler_params=pltpu.CompilerParams(vmem_limit_bytes=16 * 2**20),
    )(holder, values, grad_input, gradient, weight, first, second)


def solution(mesh):
    rows = P(("dp", "fsdp"), None)
    shard = P("fsdp", None)
    return jax.shard_map(
        on_device,
        mesh=mesh,
        in_specs=(rows, rows, shard, shard, shard, P()),
        out_specs=(rows, rows, shard, shard, shard),
        check_vma=False,
    )
```
